128 devices in a mesh: blk: 32 (over x, z, core), layer: 4 (over y).
Axes of the slice: x: 4, y: 4, z: 4, core: 2. Of those that a mesh axis runs over, the one named last changes fastest.
Arguments:
- tile_values: bfloat16 [64, 4, 4, 128, 128], P('blk', 'layer'), may hold values from 0 to 10, as said below
- band_rows: int32 [64, 4, 4], P('blk', 'layer'), may hold values from 0 to 15, as said below
- kept_rows: int32 [64, 4, 4], P('blk', 'layer'), may hold values from 0 to 15, as said below
- prune_mask: int32 [64, 4, 128], P('blk'), may hold values 0 or 1
Outputs:
- kept: bfloat16 [64, 4, 4, 128, 128], P('blk', None, 'layer')
The draws below stay inside these ranges and needn't reach their ends.
Inputs may be any that keep to these rules, and one draw needn't show every extreme that they name: `tile_values`: positive tile entries. `band_rows`: within each column panel and band the 4 block rows are distinct. `kept_rows`: within each column panel and band the 4 kept block rows are distinct.
All inputs are finite; a program needn't handle non-finite values. No bound on the sum of `prune_mask` on one device may be relied on, other than what follows from the above.
Results may differ from the reference program's by a relative error of at most 0.001.
Values may be sent and summed in bfloat16 or wider, within the bound.
No kernel may reach another device: no remote copies, remote signals or barrier semaphores. Data moves between devices by JAX's collectives and lax.ppermute only.
A program may use at most 192 MiB of HBM per device.

```python
import math
import jax
import jax.numpy as jnp

TILE = 128
NB = 64
NQ = 4
RQ = 16
KQ = 4
KOQ = 4


def pattern_of(key):
    inner = jax.random.fold_in(key, 11)
    subkeys = jax.random.split(inner, NB * NQ)
    orders = jax.vmap(lambda one: jax.random.permutation(one, RQ))(subkeys)
    return orders[:, :KQ].reshape(NB, NQ, KQ).astype(jnp.int32)


def draw_band_rows(key, part):
    pattern = pattern_of(key)
    return pattern


def draw_tile_values(key, part):
    pattern = pattern_of(key)
    key = jax.random.fold_in(key, 5)
    scale_key, base_key = jax.random.split(key)
    band_ids = jnp.arange(NQ, dtype=jnp.float32)
    growth = jnp.sqrt(1.0 + 2.0 * band_ids / max(NQ - 1, 1))
    row_power = jax.random.uniform(scale_key, (NQ, RQ, TILE))
    chosen = row_power[jnp.arange(NQ)[None, :, None], pattern]
    row_scale = jnp.power(10.0, 0.5 * chosen)
    shape = (NB, NQ, KQ, TILE, TILE)
    magnitude = jnp.exp(-math.log(1000.0) * jax.random.uniform(base_key, shape))
    values = magnitude * row_scale[..., None] * growth[None, :, None, None, None]
    return values.astype(jnp.bfloat16)


def draw_kept_rows(key, part):
    key = jax.random.fold_in(key, 7)
    subkeys = jax.random.split(key, NB * NQ)
    orders = jax.vmap(lambda one: jax.random.permutation(one, RQ))(subkeys)
    return orders[:, :KOQ].reshape(NB, NQ, KOQ).astype(jnp.int32)


def plant(result, stream_key, smallest, top_value):
    dims = result.shape
    spot = [jax.random.randint(jax.random.fold_in(stream_key, axis), (), 0, dims[axis]) for axis in range(len(dims))]
    result = result.at[tuple(spot)].set(smallest)
    longest = dims.index(max(dims))
    spot[longest] = (spot[longest] + 1) % dims[longest]
    return result.at[tuple(spot)].set(top_value)


def setup_inputs(seed: int = 0) -> dict:
    key_of = jax.random.split(jax.random.key(seed), 5)
    tile_values = draw_tile_values(jax.random.fold_in(key_of[4], 71), 0)
    band_rows = draw_band_rows(jax.random.fold_in(key_of[4], 71), 0)
    kept_rows = draw_kept_rows(jax.random.fold_in(key_of[4], 71), 0)
    prune_mask = plant((jax.random.randint(key_of[3], (NB, NQ, TILE), 0, 4) < 3).astype(jnp.int32), jax.random.fold_in(key_of[3], 1), 0, 1)
    return {"tile_values": tile_values, "band_rows": band_rows, "kept_rows": kept_rows, "prune_mask": prune_mask}


def reference(tile_values, band_rows, kept_rows, prune_mask):
    row_count = NB * TILE
    panel_ids = jnp.arange(NB, dtype=jnp.int32)[:, None, None]
    band_ids = jnp.arange(NQ, dtype=jnp.int32)[None, :, None]
    block_ids = band_ids * RQ + band_rows
    tiled = jnp.zeros((NB, NB, TILE, TILE), jnp.bfloat16)
    tiled = tiled.at[block_ids, jnp.broadcast_to(panel_ids, block_ids.shape)].set(tile_values)
    matrix = tiled.transpose(0, 2, 1, 3).reshape(row_count, row_count)
    expanded = jnp.dot(matrix, matrix, preferred_element_type=jnp.float32)
    squared = expanded * expanded
    totals = jnp.sum(squared, axis=0)
    scaled = (squared * (row_count / totals)).astype(jnp.bfloat16)
    blocked = scaled.reshape(NB, TILE, NB, TILE)
    kept_blocks = band_ids * RQ + kept_rows
    picked = blocked[kept_blocks, :, jnp.broadcast_to(panel_ids, kept_blocks.shape), :]
    keep_mask = prune_mask[:, :, None, None, :].astype(jnp.bfloat16)
    return picked * keep_mask
```

```python
import functools

import jax
import jax.numpy as jnp
from jax import lax
from jax.experimental import pallas as pl
from jax.experimental.pallas import tpu as pltpu
from jax.sharding import Mesh, PartitionSpec as P

TILE = 128
SLOTS = 4
PANELS = 2
BANDS = 4
BLOCKS = 16
COLUMNS = 64
BODY = PANELS * SLOTS * TILE
UNIT = BODY + 16
CHUNK = PANELS * TILE + 8
CELL = ("x", "z", "core")
VMEM = pl.BlockSpec(memory_space=pltpu.VMEM)
SMEM = pl.BlockSpec(memory_space=pltpu.SMEM)
LIMIT = pltpu.CompilerParams(vmem_limit_bytes=40 * 1024 * 1024)


def ring(shift):
    return [(i, (i + shift) % 4) for i in range(4)]


def cells(first, second):
    pairs = []
    for x in range(4):
        for z in range(4):
            for core, (dx, dz) in enumerate((first, second)):
                target = ((x + dx) % 4) * 4 + (z + dz) % 4
                pairs.append(((x * 4 + z) * 2 + core, target * 2 + core))
    return pairs


def pack_kernel(rows_ref, tiles_ref, unit_ref):
    band = lax.axis_index("layer")
    cell = (lax.axis_index("x") * 4 + lax.axis_index("z")) * 2 + lax.axis_index("core")
    unit_ref[:BODY] = tiles_ref[...].reshape(BODY, TILE)
    lane = lax.broadcasted_iota(jnp.int32, (16, TILE), 1)
    ids = jnp.zeros((16, TILE), jnp.int32)
    for j in range(PANELS):
        for k in range(SLOTS):
            ids = jnp.where(lane == 8 * j + k, rows_ref[j, 0, k] + BLOCKS * band, ids)
        ids = jnp.where(lane == 8 * j + 4, cell * PANELS + j, ids)
    unit_ref[BODY:] = ids.astype(jnp.float32).astype(jnp.bfloat16)


def expand_kernel(lefts, kept_ref, *refs):
    left_refs, right_refs = refs[:lefts], refs[lefts : lefts + BANDS]
    chunk_refs = refs[lefts + BANDS : lefts + 2 * BANDS]
    acc, right, wide, ids, where, sem = refs[lefts + 2 * BANDS :]
    band = lax.axis_index("layer")

    for a, ref in enumerate(left_refs):
        for u in range(4):
            row = ref[u * UNIT + BODY : (u + 1) * UNIT].astype(jnp.float32).astype(jnp.int32)
            wide[pl.ds(a * 4 + u, 1)] = row[:1]
    for b, ref in enumerate(right_refs):
        row = ref[BODY:].astype(jnp.float32).astype(jnp.int32)
        wide[pl.ds(lefts * 4 + b, 1)] = row[:1]
        for p in range(PANELS):
            right[p, pl.ds(b * SLOTS, SLOTS)] = ref[p * SLOTS * TILE : (p + 1) * SLOTS * TILE].reshape(SLOTS, TILE, TILE)
    copy = pltpu.make_async_copy(wide, ids, sem)
    copy.start()
    acc[...] = jnp.zeros_like(acc)
    copy.wait()

    for p in range(PANELS):
        for j in range(COLUMNS):
            where[p, j] = -1
    for p in range(PANELS):
        for b in range(BANDS):
            for k in range(SLOTS):
                where[p, ids[lefts * 4 + b, 8 * p + k]] = b * SLOTS + k

    for a, ref in enumerate(left_refs):

        def step(i, carry, a=a, ref=ref):
            unit = a * 4 + i // PANELS
            j = lax.rem(i, PANELS)
            column = ids[unit, 8 * j + 4]
            start = pl.multiple_of((i // PANELS) * UNIT + j * SLOTS * TILE, 16)
            for p in range(PANELS):
                slot = where[p, column]

                @pl.when(slot >= 0)
                def _():
                    product = jnp.dot(
                        ref[pl.ds(start, SLOTS * TILE)], right[p, slot], preferred_element_type=jnp.float32
                    )
                    for k in range(SLOTS):
                        block = ids[unit, 8 * j + k] - BLOCKS * band
                        acc[p, block] += product[k * TILE : (k + 1) * TILE]

            return carry

        lax.fori_loop(0, 4 * PANELS, step, 0)

    for p in range(PANELS):

        def add(r, total):
            value = acc[p, r]
            return total + jnp.sum((value * value).reshape(TILE // 8, 8, TILE), axis=0)

        total = lax.fori_loop(0, BLOCKS, add, jnp.zeros((8, TILE), jnp.float32))
        total = jnp.sum(total, axis=0, keepdims=True)
        for s in range(BANDS):
            slot = lax.rem(band + s, BANDS)
            value = acc[p, kept_ref[p, 0, slot]]
            chunk_refs[s][p * TILE : (p + 1) * TILE] = value * value
            chunk_refs[s][PANELS * TILE + 4 * p : PANELS * TILE + 4 * p + 4] = jnp.broadcast_to(total, (4, TILE))


def finish_kernel(mask_ref, *refs):
    chunk_refs, out_ref = refs[:BANDS], refs[BANDS]
    band = lax.axis_index("layer")
    for p in range(PANELS):
        row = PANELS * TILE + 4 * p
        total = sum(ref[row : row + 1] for ref in chunk_refs)
        scale = (COLUMNS * TILE) / total
        for s in range(BANDS):
            source = lax.rem(band - s + BANDS, BANDS)
            keep = mask_ref[p, pl.ds(source, 1)].astype(jnp.float32).astype(jnp.bfloat16)
            value = (chunk_refs[s][p * TILE : (p + 1) * TILE] * scale).astype(jnp.bfloat16)
            out_ref[p, source, 0] = value * keep


def per_device(tile_values, band_rows, kept_rows, prune_mask):
    unit = pl.pallas_call(
        pack_kernel,
        out_shape=jax.ShapeDtypeStruct((UNIT, TILE), jnp.bfloat16),
        in_specs=[SMEM, VMEM],
        out_specs=VMEM,
        compiler_params=LIMIT,
    )(band_rows, tile_values)

    lines = [lax.ppermute(unit, CELL, cells(a, b)) for a, b in (((1, 0), (0, 1)), ((3, 0), (0, 3)), ((2, 0), (0, 2)))]
    line = jnp.concatenate([unit, *lines], axis=0)
    rights = [unit] + [lax.ppermute(unit, "layer", ring(s)) for s in (1, 3, 2)]
    rest = [lax.ppermute(line, CELL, cells(a, b)) for a, b in (((0, 1), (1, 0)), ((0, 3), (3, 0)), ((0, 2), (2, 0)))]
    lefts = [line, *rest]
    lefts = lefts + [lax.ppermute(one, "core", [(0, 1), (1, 0)]) for one in lefts]

    count = len(lefts)
    ids = count * 4 + 8
    chunks = pl.pallas_call(
        functools.partial(expand_kernel, count),
        out_shape=[jax.ShapeDtypeStruct((CHUNK, TILE), jnp.float32)] * BANDS,
        in_specs=[SMEM] + [VMEM] * (count + BANDS),
        out_specs=[VMEM] * BANDS,
        scratch_shapes=[
            pltpu.VMEM((PANELS, BLOCKS, TILE, TILE), jnp.float32),
            pltpu.VMEM((PANELS, BANDS * SLOTS, TILE, TILE), jnp.bfloat16),
            pltpu.VMEM((ids, TILE), jnp.int32),
            pltpu.SMEM((ids, TILE), jnp.int32),
            pltpu.SMEM((PANELS, COLUMNS), jnp.int32),
            pltpu.SemaphoreType.DMA,
        ],
        compiler_params=LIMIT,
        cost_estimate=pl.CostEstimate(flops=2**29, bytes_accessed=10 * 2**20, transcendentals=0),
    )(kept_rows, *lefts, *rights)

    chunks = [chunks[0]] + [lax.ppermute(chunks[s], "layer", ring(s)) for s in (1, 2, 3)]
    return pl.pallas_call(
        finish_kernel,
        out_shape=jax.ShapeDtypeStruct((PANELS, BANDS, 1, TILE, TILE), jnp.bfloat16),
        in_specs=[VMEM] * (1 + BANDS),
        out_specs=VMEM,
        compiler_params=LIMIT,
    )(prune_mask, *chunks)


def solution(mesh):
    parts = Mesh(mesh.devices.reshape(4, 4, 2, 4), CELL + ("layer",))
    return jax.shard_map(
        per_device,
        mesh=parts,
        in_specs=(
            P(CELL, "layer", None, None, None),
            P(CELL, "layer", None),
            P(CELL, "layer", None),
            P(CELL, None, None),
        ),
        out_specs=P(CELL, None, "layer", None, None),
        check_vma=False,
    )
```

```python
import functools

import jax
import jax.numpy as jnp
from jax import lax
from jax.experimental import pallas as pl
from jax.experimental.pallas import tpu as pltpu
from jax.sharding import Mesh, PartitionSpec as P

TILE = 128
SLOTS = 4
PANELS = 2
BANDS = 4
BLOCKS = 16
COLUMNS = 64
LINE = 4
BODY = PANELS * SLOTS * TILE
UNIT = BODY + 16
CHUNK = PANELS * TILE + 8
CELL = ("x", "z", "core")
VMEM = pl.BlockSpec(memory_space=pltpu.VMEM)
SMEM = pl.BlockSpec(memory_space=pltpu.SMEM)
LIMIT = pltpu.CompilerParams(vmem_limit_bytes=40 * 1024 * 1024)


def ring(shift):
    return [(i, (i + shift) % 4) for i in range(4)]


def cells(first, second):
    pairs = []
    for x in range(4):
        for z in range(4):
            for core, (dx, dz) in enumerate((first, second)):
                target = ((x + dx) % 4) * 4 + (z + dz) % 4
                pairs.append(((x * 4 + z) * 2 + core, target * 2 + core))
    return pairs


def pack_kernel(rows_ref, tiles_ref, unit_ref):
    band = lax.axis_index("layer")
    cell = (lax.axis_index("x") * 4 + lax.axis_index("z")) * 2 + lax.axis_index("core")
    unit_ref[:BODY] = tiles_ref[...].reshape(BODY, TILE)
    lane = lax.broadcasted_iota(jnp.int32, (16, TILE), 1)
    ids = jnp.zeros((16, TILE), jnp.int32)
    for j in range(PANELS):
        for k in range(SLOTS):
            ids = jnp.where(lane == 8 * j + k, rows_ref[j, 0, k] + BLOCKS * band, ids)
        ids = jnp.where(lane == 8 * j + 4, cell * PANELS + j, ids)
    unit_ref[BODY:] = ids.astype(jnp.float32).astype(jnp.bfloat16)


def join_kernel(*refs):
    line_refs, right_refs, (line_ref, tiles_ref, ids_ref) = refs[:LINE], refs[LINE : LINE + BANDS], refs[LINE + BANDS :]
    for u, ref in enumerate(line_refs):
        line_ref[u * UNIT : (u + 1) * UNIT] = ref[...]
    for b, ref in enumerate(right_refs):
        ids_ref[8 * b : 8 * b + 8] = ref[BODY:].astype(jnp.float32).astype(jnp.int32)[:8]
        for p in range(PANELS):
            tiles_ref[p, b * SLOTS : (b + 1) * SLOTS] = ref[p * SLOTS * TILE : (p + 1) * SLOTS * TILE].reshape(
                SLOTS, TILE, TILE
            )


def expand_kernel(lefts, kept_ref, tiles_ref, right_ids_ref, *refs):
    left_refs, chunk_refs = refs[: len(lefts)], refs[len(lefts) : len(lefts) + BANDS]
    all_ref, acc, wide, ids, place, sem = refs[len(lefts) + BANDS :]
    band = lax.axis_index("layer")
    units = sum(lefts)

    done = 0
    for ref, count in zip(left_refs, lefts):
        all_ref[done * UNIT : (done + count) * UNIT] = ref[...]
        for u in range(count):
            row = ref[u * UNIT + BODY : (u + 1) * UNIT].astype(jnp.float32).astype(jnp.int32)
            wide[pl.ds(done + u, 1)] = row[:1]
        done += count
    for b in range(BANDS):
        wide[pl.ds(units + b, 1)] = right_ids_ref[8 * b : 8 * b + 1]
    copy = pltpu.make_async_copy(wide, ids, sem)
    copy.start()
    acc[...] = jnp.zeros_like(acc)
    copy.wait()

    def fill(u, carry):
        for j in range(PANELS):
            place[ids[u, 8 * j + 4]] = u * PANELS + j
        return carry

    lax.fori_loop(0, units, fill, 0, unroll=8)

    for p in range(PANELS):
        for s in range(BANDS * SLOTS):
            found = place[ids[units + s // SLOTS, 8 * p + s % SLOTS]]
            unit, j = found // PANELS, found % PANELS
            start = pl.multiple_of(unit * UNIT + j * SLOTS * TILE, 16)
            product = jnp.dot(
                all_ref[pl.ds(start, SLOTS * TILE)], tiles_ref[p, s], preferred_element_type=jnp.float32
            )
            for k in range(SLOTS):
                acc[p, ids[unit, 8 * j + k] % BLOCKS] += product[k * TILE : (k + 1) * TILE]

    for p in range(PANELS):

        def add(r, total):
            value = acc[p, r]
            return total + jnp.sum((value * value).reshape(TILE // 8, 8, TILE), axis=0)

        total = lax.fori_loop(0, BLOCKS, add, jnp.zeros((8, TILE), jnp.float32), unroll=4)
        total = jnp.sum(total, axis=0, keepdims=True)
        for s in range(BANDS):
            slot = lax.rem(band + s, BANDS)
            value = acc[p, kept_ref[p, 0, slot]]
            chunk_refs[s][p * TILE : (p + 1) * TILE] = value * value
            chunk_refs[s][PANELS * TILE + 4 * p : PANELS * TILE + 4 * p + 4] = jnp.broadcast_to(total, (4, TILE))


def finish_kernel(mask_ref, *refs):
    chunk_refs, out_ref = refs[:BANDS], refs[BANDS]
    band = lax.axis_index("layer")
    for p in range(PANELS):
        row = PANELS * TILE + 4 * p
        total = sum(ref[row : row + 1] for ref in chunk_refs)
        scale = (COLUMNS * TILE) / total
        for s in range(BANDS):
            source = lax.rem(band - s + BANDS, BANDS)
            keep = mask_ref[p, pl.ds(source, 1)].astype(jnp.float32).astype(jnp.bfloat16)
            value = (chunk_refs[s][p * TILE : (p + 1) * TILE] * scale).astype(jnp.bfloat16)
            out_ref[p, source, 0] = value * keep


def per_device(tile_values, band_rows, kept_rows, prune_mask):
    unit = pl.pallas_call(
        pack_kernel,
        out_shape=jax.ShapeDtypeStruct((UNIT, TILE), jnp.bfloat16),
        in_specs=[SMEM, VMEM],
        out_specs=VMEM,
        compiler_params=LIMIT,
    )(band_rows, tile_values)

    def swap(value):
        return lax.ppermute(value, "core", [(0, 1), (1, 0)])

    def swap(value):
        return lax.ppermute(value, "core", [(0, 1), (1, 0)])

    lines = [lax.ppermute(unit, CELL, cells(a, b)) for a, b in (((1, 0), (0, 1)), ((3, 0), (0, 3)), ((2, 0), (0, 2)))]
    line = jnp.concatenate([unit, *lines], axis=0)
    rights = [unit] + [lax.ppermute(unit, "layer", ring(s)) for s in (1, 3, 2)]
    up, down = [lax.ppermute(line, CELL, cells(a, b)) for a, b in (((0, 1), (1, 0)), ((0, 3), (3, 0)))]
    line_again, tiles, right_ids = pl.pallas_call(
        join_kernel,
        out_shape=[
            jax.ShapeDtypeStruct((LINE * UNIT, TILE), jnp.bfloat16),
            jax.ShapeDtypeStruct((PANELS, BANDS * SLOTS, TILE, TILE), jnp.bfloat16),
            jax.ShapeDtypeStruct((8 * BANDS, TILE), jnp.int32),
        ],
        in_specs=[VMEM] * (LINE + BANDS),
        out_specs=[VMEM] * 3,
        compiler_params=LIMIT,
    )(unit, *lines, *rights)
    far = lax.ppermute(line_again, CELL, cells((0, 2), (2, 0)))

    lefts = [line, up, down, swap(line), swap(up), swap(down), far, swap(far)]
    counts = tuple(one.shape[0] // UNIT for one in lefts)
    units = sum(counts)
    chunks = pl.pallas_call(
        functools.partial(expand_kernel, counts),
        out_shape=[jax.ShapeDtypeStruct((CHUNK, TILE), jnp.float32)] * BANDS,
        in_specs=[SMEM] + [VMEM] * (len(lefts) + 2),
        out_specs=[VMEM] * BANDS,
        scratch_shapes=[
            pltpu.VMEM((units * UNIT, TILE), jnp.bfloat16),
            pltpu.VMEM((PANELS, BLOCKS, TILE, TILE), jnp.float32),
            pltpu.VMEM((units + 8, TILE), jnp.int32),
            pltpu.SMEM((units + 8, TILE), jnp.int32),
            pltpu.SMEM((COLUMNS,), jnp.int32),
            pltpu.SemaphoreType.DMA,
        ],
        compiler_params=LIMIT,
        cost_estimate=pl.CostEstimate(flops=2**29, bytes_accessed=10 * 2**20, transcendentals=0),
    )(kept_rows, tiles, right_ids, *lefts)

    chunks = [chunks[0]] + [lax.ppermute(chunks[s], "layer", ring(s)) for s in (1, 2, 3)]
    return pl.pallas_call(
        finish_kernel,
        out_shape=jax.ShapeDtypeStruct((PANELS, BANDS, 1, TILE, TILE), jnp.bfloat16),
        in_specs=[VMEM] * (1 + BANDS),
        out_specs=VMEM,
        compiler_params=LIMIT,
    )(prune_mask, *chunks)


def solution(mesh):
    parts = Mesh(mesh.devices.reshape(4, 4, 2, 4), CELL + ("layer",))
    return jax.shard_map(
        per_device,
        mesh=parts,
        in_specs=(
            P(CELL, "layer", None, None, None),
            P(CELL, "layer", None),
            P(CELL, "layer", None),
            P(CELL, None, None),
        ),
        out_specs=P(CELL, None, "layer", None, None),
        check_vma=False,
    )
```

```python
import functools

import jax
import jax.numpy as jnp
from jax import lax
from jax.experimental import pallas as pl
from jax.experimental.pallas import tpu as pltpu
from jax.sharding import Mesh, PartitionSpec as P

TILE = 128
SLOTS = 4
PANELS = 2
BANDS = 4
BLOCKS = 16
COLUMNS = 64
LINE = 4
BODY = PANELS * SLOTS * TILE
UNIT = BODY + 16
CHUNK = PANELS * TILE + 8
CELL = ("x", "z", "core")
VMEM = pl.BlockSpec(memory_space=pltpu.VMEM)
SMEM = pl.BlockSpec(memory_space=pltpu.SMEM)
LIMIT = pltpu.CompilerParams(vmem_limit_bytes=40 * 1024 * 1024)


def ring(shift):
    return [(i, (i + shift) % 4) for i in range(4)]


def cells(first, second):
    pairs = []
    for x in range(4):
        for z in range(4):
            for core, (dx, dz) in enumerate((first, second)):
                target = ((x + dx) % 4) * 4 + (z + dz) % 4
                pairs.append(((x * 4 + z) * 2 + core, target * 2 + core))
    return pairs


def pack_kernel(rows_ref, tiles_ref, unit_ref):
    band = lax.axis_index("layer")
    cell = (lax.axis_index("x") * 4 + lax.axis_index("z")) * 2 + lax.axis_index("core")
    unit_ref[:BODY] = tiles_ref[...].reshape(BODY, TILE)
    lane = lax.broadcasted_iota(jnp.int32, (16, TILE), 1)
    ids = jnp.zeros((16, TILE), jnp.int32)
    for j in range(PANELS):
        for k in range(SLOTS):
            ids = jnp.where(lane == 8 * j + k, rows_ref[j, 0, k] + BLOCKS * band, ids)
        ids = jnp.where(lane == 8 * j + 4, cell * PANELS + j, ids)
    unit_ref[BODY:] = ids.astype(jnp.float32).astype(jnp.bfloat16)


def again_kernel(unit_ref, *refs):
    refs[-1][...] = unit_ref[...]


def join_kernel(*refs):
    line_refs, right_refs, (line_ref, tiles_ref, ids_ref) = refs[:LINE], refs[LINE : LINE + BANDS], refs[LINE + BANDS :]
    for u, ref in enumerate(line_refs):
        line_ref[u * UNIT : (u + 1) * UNIT] = ref[...]
    for b, ref in enumerate(right_refs):
        ids_ref[8 * b : 8 * b + 8] = ref[BODY:].astype(jnp.float32).astype(jnp.int32)[:8]
        for p in range(PANELS):
            tiles_ref[p, b * SLOTS : (b + 1) * SLOTS] = ref[p * SLOTS * TILE : (p + 1) * SLOTS * TILE].reshape(
                SLOTS, TILE, TILE
            )


def expand_kernel(lefts, kept_ref, tiles_ref, right_ids_ref, *refs):
    left_refs, chunk_refs = refs[: len(lefts)], refs[len(lefts) : len(lefts) + BANDS]
    all_ref, acc, wide, ids, place, sem = refs[len(lefts) + BANDS :]
    band = lax.axis_index("layer")
    units = sum(lefts)

    done = 0
    for ref, count in zip(left_refs, lefts):
        all_ref[done * UNIT : (done + count) * UNIT] = ref[...]
        for u in range(count):
            row = ref[u * UNIT + BODY : (u + 1) * UNIT].astype(jnp.float32).astype(jnp.int32)
            wide[pl.ds(done + u, 1)] = row[:1]
        done += count
    for b in range(BANDS):
        wide[pl.ds(units + b, 1)] = right_ids_ref[8 * b : 8 * b + 1]
    copy = pltpu.make_async_copy(wide, ids, sem)
    copy.start()
    acc[...] = jnp.zeros_like(acc)
    copy.wait()

    def fill(u, carry):
        for j in range(PANELS):
            place[ids[u, 8 * j + 4]] = u * PANELS + j
        return carry

    lax.fori_loop(0, units, fill, 0, unroll=8)

    for p in range(PANELS):
        for s in range(BANDS * SLOTS):
            found = place[ids[units + s // SLOTS, 8 * p + s % SLOTS]]
            unit, j = found // PANELS, found % PANELS
            start = pl.multiple_of(unit * UNIT + j * SLOTS * TILE, 16)
            product = jnp.dot(
                all_ref[pl.ds(start, SLOTS * TILE)], tiles_ref[p, s], preferred_element_type=jnp.float32
            )
            for k in range(SLOTS):
                acc[p, ids[unit, 8 * j + k] % BLOCKS] += product[k * TILE : (k + 1) * TILE]

    for p in range(PANELS):

        def add(r, total):
            value = acc[p, r]
            return total + jnp.sum((value * value).reshape(TILE // 8, 8, TILE), axis=0)

        total = lax.fori_loop(0, BLOCKS, add, jnp.zeros((8, TILE), jnp.float32), unroll=4)
        total = jnp.sum(total, axis=0, keepdims=True)
        for s in range(BANDS):
            slot = lax.rem(band + s, BANDS)
            value = acc[p, kept_ref[p, 0, slot]]
            chunk_refs[s][p * TILE : (p + 1) * TILE] = value * value
            chunk_refs[s][PANELS * TILE + 4 * p : PANELS * TILE + 4 * p + 4] = jnp.broadcast_to(total, (4, TILE))


def finish_kernel(mask_ref, *refs):
    chunk_refs, out_ref = refs[:BANDS], refs[BANDS]
    band = lax.axis_index("layer")
    for p in range(PANELS):
        row = PANELS * TILE + 4 * p
        total = sum(ref[row : row + 1] for ref in chunk_refs)
        scale = (COLUMNS * TILE) / total
        for s in range(BANDS):
            source = lax.rem(band - s + BANDS, BANDS)
            keep = mask_ref[p, pl.ds(source, 1)].astype(jnp.float32).astype(jnp.bfloat16)
            value = (chunk_refs[s][p * TILE : (p + 1) * TILE] * scale).astype(jnp.bfloat16)
            out_ref[p, source, 0] = value * keep


def per_device(tile_values, band_rows, kept_rows, prune_mask):
    unit = pl.pallas_call(
        pack_kernel,
        out_shape=jax.ShapeDtypeStruct((UNIT, TILE), jnp.bfloat16),
        in_specs=[SMEM, VMEM],
        out_specs=VMEM,
        compiler_params=LIMIT,
    )(band_rows, tile_values)

    def swap(value):
        return lax.ppermute(value, "core", [(0, 1), (1, 0)])

    def swap(value):
        return lax.ppermute(value, "core", [(0, 1), (1, 0)])

    lines = [lax.ppermute(unit, CELL, cells(a, b)) for a, b in (((1, 0), (0, 1)), ((3, 0), (0, 3)), ((2, 0), (0, 2)))]
    line = jnp.concatenate([unit, *lines], axis=0)
    unit_again = pl.pallas_call(
        again_kernel,
        out_shape=jax.ShapeDtypeStruct((UNIT, TILE), jnp.bfloat16),
        in_specs=[VMEM] * LINE,
        out_specs=VMEM,
        compiler_params=LIMIT,
    )(unit, *lines)
    rights = [unit] + [lax.ppermute(unit_again, "layer", ring(s)) for s in (1, 3, 2)]
    up, down = [lax.ppermute(line, CELL, cells(a, b)) for a, b in (((0, 1), (1, 0)), ((0, 3), (3, 0)))]
    line_again, tiles, right_ids = pl.pallas_call(
        join_kernel,
        out_shape=[
            jax.ShapeDtypeStruct((LINE * UNIT, TILE), jnp.bfloat16),
            jax.ShapeDtypeStruct((PANELS, BANDS * SLOTS, TILE, TILE), jnp.bfloat16),
            jax.ShapeDtypeStruct((8 * BANDS, TILE), jnp.int32),
        ],
        in_specs=[VMEM] * (LINE + BANDS),
        out_specs=[VMEM] * 3,
        compiler_params=LIMIT,
    )(unit, *lines, *rights)
    far = lax.ppermute(line, CELL, cells((0, 2), (2, 0)))

    lefts = [line, up, down, swap(line_again), swap(up), swap(down), far, swap(far)]
    counts = tuple(one.shape[0] // UNIT for one in lefts)
    units = sum(counts)
    chunks = pl.pallas_call(
        functools.partial(expand_kernel, counts),
        out_shape=[jax.ShapeDtypeStruct((CHUNK, TILE), jnp.float32)] * BANDS,
        in_specs=[SMEM] + [VMEM] * (len(lefts) + 2),
        out_specs=[VMEM] * BANDS,
        scratch_shapes=[
            pltpu.VMEM((units * UNIT, TILE), jnp.bfloat16),
            pltpu.VMEM((PANELS, BLOCKS, TILE, TILE), jnp.float32),
            pltpu.VMEM((units + 8, TILE), jnp.int32),
            pltpu.SMEM((units + 8, TILE), jnp.int32),
            pltpu.SMEM((COLUMNS,), jnp.int32),
            pltpu.SemaphoreType.DMA,
        ],
        compiler_params=LIMIT,
        cost_estimate=pl.CostEstimate(flops=2**29, bytes_accessed=10 * 2**20, transcendentals=0),
    )(kept_rows, tiles, right_ids, *lefts)

    chunks = [chunks[0]] + [lax.ppermute(chunks[s], "layer", ring(s)) for s in (1, 2, 3)]
    return pl.pallas_call(
        finish_kernel,
        out_shape=jax.ShapeDtypeStruct((PANELS, BANDS, 1, TILE, TILE), jnp.bfloat16),
        in_specs=[VMEM] * (1 + BANDS),
        out_specs=VMEM,
        compiler_params=LIMIT,
    )(prune_mask, *chunks)


def solution(mesh):
    parts = Mesh(mesh.devices.reshape(4, 4, 2, 4), CELL + ("layer",))
    return jax.shard_map(
        per_device,
        mesh=parts,
        in_specs=(
            P(CELL, "layer", None, None, None),
            P(CELL, "layer", None),
            P(CELL, "layer", None),
            P(CELL, None, None),
        ),
        out_specs=P(CELL, None, "layer", None, None),
        check_vma=False,
    )
```

```python
import functools

import jax
import jax.numpy as jnp
from jax import lax
from jax.experimental import pallas as pl
from jax.experimental.pallas import tpu as pltpu
from jax.sharding import Mesh, PartitionSpec as P

TILE = 128
SLOTS = 4
PANELS = 2
BANDS = 4
BLOCKS = 16
COLUMNS = 64
LINE = 4
BODY = PANELS * SLOTS * TILE
UNIT = BODY + 16
CHUNK = PANELS * TILE + 8
CELL = ("x", "z", "core")
VMEM = pl.BlockSpec(memory_space=pltpu.VMEM)
HBM = pl.BlockSpec(memory_space=pltpu.HBM)
SMEM = pl.BlockSpec(memory_space=pltpu.SMEM)
LIMIT = pltpu.CompilerParams(vmem_limit_bytes=40 * 1024 * 1024)


def ring(shift):
    return [(i, (i + shift) % 4) for i in range(4)]


def cells(first, second):
    pairs = []
    for x in range(4):
        for z in range(4):
            for core, (dx, dz) in enumerate((first, second)):
                target = ((x + dx) % 4) * 4 + (z + dz) % 4
                pairs.append(((x * 4 + z) * 2 + core, target * 2 + core))
    return pairs


def pack_kernel(rows_ref, tiles_ref, unit_ref, rows, sems):
    tiles_copies = [
        pltpu.make_async_copy(
            tiles_ref.at[j, 0, k], unit_ref.at[pl.ds((j * SLOTS + k) * TILE, TILE)], sems.at[j * SLOTS + k]
        )
        for j in range(PANELS)
        for k in range(SLOTS)
    ]
    rows_copy = pltpu.make_async_copy(rows_ref, rows, sems.at[PANELS * SLOTS])
    rows_copy.start()
    for copy in tiles_copies:
        copy.start()
    band = lax.axis_index("layer")
    cell = (lax.axis_index("x") * 4 + lax.axis_index("z")) * 2 + lax.axis_index("core")
    lane = lax.broadcasted_iota(jnp.int32, (16, TILE), 1)
    ids = jnp.zeros((16, TILE), jnp.int32)
    for j in range(PANELS):
        ids = jnp.where(lane == 8 * j + 4, cell * PANELS + j, ids)
    rows_copy.wait()
    for j in range(PANELS):
        for k in range(SLOTS):
            ids = jnp.where(lane == 8 * j + k, rows[j, 0, k] + BLOCKS * band, ids)
    unit_ref[BODY:] = ids.astype(jnp.float32).astype(jnp.bfloat16)
    for copy in tiles_copies:
        copy.wait()


def second_kernel(*refs):
    unit_ref, one_ref, other_ref = refs[:3]
    second_ref, again_ref = refs[-2:]
    second_ref[:UNIT] = one_ref[...]
    second_ref[UNIT:] = other_ref[...]
    again_ref[...] = unit_ref[...]


def join_kernel(count, *refs):
    line_refs, right_refs = refs[:count], refs[count : count + BANDS]
    line_ref, tiles_ref, ids_ref = refs[count + BANDS :]
    done = 0
    for ref in line_refs:
        line_ref[done : done + ref.shape[0]] = ref[...]
        done += ref.shape[0]
    for b, ref in enumerate(right_refs):
        ids_ref[8 * b : 8 * b + 8] = ref[BODY:].astype(jnp.float32).astype(jnp.int32)[:8]
        for p in range(PANELS):
            tiles_ref[p, b * SLOTS : (b + 1) * SLOTS] = ref[p * SLOTS * TILE : (p + 1) * SLOTS * TILE].reshape(
                SLOTS, TILE, TILE
            )


def expand_kernel(lefts, kept_ref, tiles_ref, right_ids_ref, *refs):
    left_refs, chunk_refs = refs[: len(lefts)], refs[len(lefts) : len(lefts) + BANDS]
    all_ref, acc, wide, ids, place, sem = refs[len(lefts) + BANDS :]
    band = lax.axis_index("layer")
    units = sum(lefts)

    done = 0
    for ref, count in zip(left_refs, lefts):
        all_ref[done * UNIT : (done + count) * UNIT] = ref[...]
        for u in range(count):
            row = ref[u * UNIT + BODY : (u + 1) * UNIT].astype(jnp.float32).astype(jnp.int32)
            wide[pl.ds(done + u, 1)] = row[:1]
        done += count
    for b in range(BANDS):
        wide[pl.ds(units + b, 1)] = right_ids_ref[8 * b : 8 * b + 1]
    copy = pltpu.make_async_copy(wide, ids, sem)
    copy.start()
    acc[...] = jnp.zeros_like(acc)
    copy.wait()

    def fill(u, carry):
        for j in range(PANELS):
            place[ids[u, 8 * j + 4]] = u * PANELS + j
        return carry

    lax.fori_loop(0, units, fill, 0, unroll=8)

    for p in range(PANELS):
        for s in range(BANDS * SLOTS):
            found = place[ids[units + s // SLOTS, 8 * p + s % SLOTS]]
            unit, j = found // PANELS, found % PANELS
            start = pl.multiple_of(unit * UNIT + j * SLOTS * TILE, 16)
            product = jnp.dot(
                all_ref[pl.ds(start, SLOTS * TILE)], tiles_ref[p, s], preferred_element_type=jnp.float32
            )
            for k in range(SLOTS):
                acc[p, ids[unit, 8 * j + k] % BLOCKS] += product[k * TILE : (k + 1) * TILE]

    for p in range(PANELS):

        def add(r, total):
            value = acc[p, r]
            return total + jnp.sum((value * value).reshape(TILE // 8, 8, TILE), axis=0)

        total = lax.fori_loop(0, BLOCKS, add, jnp.zeros((8, TILE), jnp.float32), unroll=4)
        total = jnp.sum(total, axis=0, keepdims=True)
        for s in range(BANDS):
            slot = lax.rem(band + s, BANDS)
            value = acc[p, kept_ref[p, 0, slot]]
            chunk_refs[s][p * TILE : (p + 1) * TILE] = value * value
            chunk_refs[s][PANELS * TILE + 4 * p : PANELS * TILE + 4 * p + 4] = jnp.broadcast_to(total, (4, TILE))


def finish_kernel(mask_ref, *refs):
    chunk_refs, out_ref = refs[:BANDS], refs[BANDS]
    band = lax.axis_index("layer")
    for p in range(PANELS):
        row = PANELS * TILE + 4 * p
        total = sum(ref[row : row + 1] for ref in chunk_refs)
        scale = (COLUMNS * TILE) / total
        for s in range(BANDS):
            source = lax.rem(band - s + BANDS, BANDS)
            keep = mask_ref[p, pl.ds(source, 1)].astype(jnp.float32).astype(jnp.bfloat16)
            value = (chunk_refs[s][p * TILE : (p + 1) * TILE] * scale).astype(jnp.bfloat16)
            out_ref[p, source, 0] = value * keep


def per_device(tile_values, band_rows, kept_rows, prune_mask):
    unit = pl.pallas_call(
        pack_kernel,
        out_shape=jax.ShapeDtypeStruct((UNIT, TILE), jnp.bfloat16),
        in_specs=[HBM, HBM],
        out_specs=VMEM,
        scratch_shapes=[
            pltpu.SMEM((PANELS, 1, SLOTS), jnp.int32),
            pltpu.SemaphoreType.DMA((PANELS * SLOTS + 1,)),
        ],
        compiler_params=LIMIT,
    )(band_rows, tile_values)

    def swap(value):
        return lax.ppermute(value, "core", [(0, 1), (1, 0)])

    def along(value, axis, shift):
        steps = ((shift, 0), (0, shift))
        return lax.ppermute(value, CELL, cells(steps[axis], steps[1 - axis]))

    near, back, away = [along(unit, 0, shift) for shift in (2, 1, 3)]
    first = jnp.concatenate([unit, near], axis=0)
    rights = [lax.ppermute(unit, "layer", ring(s)) for s in (1, 3)]
    second, unit_again = pl.pallas_call(
        second_kernel,
        out_shape=[jax.ShapeDtypeStruct((n * UNIT, TILE), jnp.bfloat16) for n in (2, 1)],
        in_specs=[VMEM] * (3 + 2),
        out_specs=[VMEM] * 2,
        compiler_params=LIMIT,
    )(unit, back, away, *rights)
    rights = [unit, *rights, lax.ppermute(unit_again, "layer", ring(2))]
    line_again, tiles, right_ids = pl.pallas_call(
        functools.partial(join_kernel, 2),
        out_shape=[
            jax.ShapeDtypeStruct((LINE * UNIT, TILE), jnp.bfloat16),
            jax.ShapeDtypeStruct((PANELS, BANDS * SLOTS, TILE, TILE), jnp.bfloat16),
            jax.ShapeDtypeStruct((8 * BANDS, TILE), jnp.int32),
        ],
        in_specs=[VMEM] * (2 + BANDS),
        out_specs=[VMEM] * 3,
        compiler_params=LIMIT,
    )(first, second, *rights)
    up, down = along(first, 1, 1), along(first, 1, 3)
    up_b, down_b = along(second, 1, 1), along(second, 1, 3)
    fars = [along(up[:UNIT], 1, 1), along(down[UNIT:], 1, 3)]
    fars_b = [along(up_b[:UNIT], 1, 1), along(down_b[UNIT:], 1, 3)]
    parts = [*fars_b, *fars, up_b, down_b, up, down]
    lefts = [first, second, *parts, swap(line_again), *[swap(one) for one in parts]]
    counts = tuple(one.shape[0] // UNIT for one in lefts)
    units = sum(counts)
    chunks = pl.pallas_call(
        functools.partial(expand_kernel, counts),
        out_shape=[jax.ShapeDtypeStruct((CHUNK, TILE), jnp.float32)] * BANDS,
        in_specs=[SMEM] + [VMEM] * (len(lefts) + 2),
        out_specs=[VMEM] * BANDS,
        scratch_shapes=[
            pltpu.VMEM((units * UNIT, TILE), jnp.bfloat16),
            pltpu.VMEM((PANELS, BLOCKS, TILE, TILE), jnp.float32),
            pltpu.VMEM((units + 8, TILE), jnp.int32),
            pltpu.SMEM((units + 8, TILE), jnp.int32),
            pltpu.SMEM((COLUMNS,), jnp.int32),
            pltpu.SemaphoreType.DMA,
        ],
        compiler_params=LIMIT,
        cost_estimate=pl.CostEstimate(flops=2**29, bytes_accessed=10 * 2**20, transcendentals=0),
    )(kept_rows, tiles, right_ids, *lefts)

    chunks = [chunks[0]] + [lax.ppermute(chunks[s], "layer", ring(s)) for s in (1, 2, 3)]
    return pl.pallas_call(
        finish_kernel,
        out_shape=jax.ShapeDtypeStruct((PANELS, BANDS, 1, TILE, TILE), jnp.bfloat16),
        in_specs=[VMEM] * (1 + BANDS),
        out_specs=VMEM,
        compiler_params=LIMIT,
    )(prune_mask, *chunks)


def solution(mesh):
    parts = Mesh(mesh.devices.reshape(4, 4, 2, 4), CELL + ("layer",))
    return jax.shard_map(
        per_device,
        mesh=parts,
        in_specs=(
            P(CELL, "layer", None, None, None),
            P(CELL, "layer", None),
            P(CELL, "layer", None),
            P(CELL, None, None),
        ),
        out_specs=P(CELL, None, "layer", None, None),
        check_vma=False,
    )
```

```python
import functools

import jax
import jax.numpy as jnp
from jax import lax
from jax.experimental import pallas as pl
from jax.experimental.pallas import tpu as pltpu
from jax.sharding import Mesh, PartitionSpec as P

TILE = 128
SLOTS = 4
PANELS = 2
BANDS = 4
BLOCKS = 16
SIDE = 4
BODY = PANELS * SLOTS * TILE
UNIT = BODY + 16
CHUNK = PANELS * TILE + 8
GROUP = 8
LANES = TILE // GROUP
CELL = ("x", "z", "core")
VMEM = pl.BlockSpec(memory_space=pltpu.VMEM)
SMEM = pl.BlockSpec(memory_space=pltpu.SMEM)
LIMIT = pltpu.CompilerParams(vmem_limit_bytes=40 * 1024 * 1024)


def ring(shift):
    return [(i, (i + shift) % SIDE) for i in range(SIDE)]


def cells(first, second):
    pairs = []
    for x in range(SIDE):
        for z in range(SIDE):
            for core, (dx, dz) in enumerate((first, second)):
                target = ((x + dx) % SIDE) * SIDE + (z + dz) % SIDE
                pairs.append(((x * SIDE + z) * 2 + core, target * 2 + core))
    return pairs


def along(value, axis, shift):
    steps = ((shift, 0), (0, shift))
    return lax.ppermute(value, CELL, cells(steps[axis], steps[1 - axis]))


def swap(value):
    return lax.ppermute(value, "core", [(0, 1), (1, 0)])


def cell_number(x, z, core):
    return (x * SIDE + z) * 2 + core


def id_rows(band_rows):
    cell = cell_number(*(lax.axis_index(name) for name in CELL))
    rows = jnp.pad(band_rows[:, 0], ((0, 0), (0, GROUP - SLOTS))).reshape(1, LANES)
    row = lax.broadcasted_iota(jnp.int32, (16, TILE), 0)
    group = lax.broadcasted_iota(jnp.int32, (16, TILE), 1) // LANES
    here = ((row == cell // GROUP) & (group == cell % GROUP)) | ((row == GROUP) & (group == 0))
    return jnp.where(here, jnp.tile(rows, (1, GROUP)), 0).astype(jnp.bfloat16)


def buffer_kernel(count, *refs):
    unit_refs, (buffer_ref, again_ref) = refs[:count], refs[-2:]
    for u, ref in enumerate(unit_refs[1:] if count == 3 else unit_refs):
        buffer_ref[u * UNIT : (u + 1) * UNIT] = ref[...]
    again_ref[...] = unit_refs[0][...]


def join_kernel(count, *refs):
    line_refs, right_refs = refs[:count], refs[count : count + BANDS]
    line_ref, tiles_ref, ids_ref = refs[count + BANDS :]
    done = 0
    for ref in line_refs:
        line_ref[done : done + ref.shape[0]] = ref[...]
        done += ref.shape[0]
    for b, ref in enumerate(right_refs):
        ids_ref[b : b + 1] = ref[BODY:].astype(jnp.float32).astype(jnp.int32)[GROUP : GROUP + 1]
        for p in range(PANELS):
            tiles_ref[p, b * SLOTS : (b + 1) * SLOTS] = ref[p * SLOTS * TILE : (p + 1) * SLOTS * TILE].reshape(
                SLOTS, TILE, TILE
            )


def expand_kernel(origins, right_shifts, chunk_shifts, kept_ref, tiles_ref, right_ids_ref, *refs):
    left_refs, chunk_refs = refs[: len(origins)], refs[len(origins) : len(origins) + BANDS]
    all_ref, acc, table, ids, place, sem = refs[len(origins) + BANDS :]
    band, x, z, core = (lax.axis_index(name) for name in ("layer",) + CELL)

    sums, done = None, 0
    for ref, units in zip(left_refs, origins):
        for u in range(len(units)):
            block = ref[u * UNIT + BODY : (u + 1) * UNIT].astype(jnp.float32)
            sums = block if sums is None else sums + block
    table[: BANDS] = sums.astype(jnp.int32)[: BANDS]
    table[BANDS : 2 * BANDS] = right_ids_ref[...]
    copy = pltpu.make_async_copy(table, ids, sem)
    copy.start()
    for ref, units in zip(left_refs, origins):
        all_ref[done * UNIT : (done + len(units)) * UNIT] = ref[...]
        for u, (one, other, across) in enumerate(units):
            owner = 1 - core if across else core
            dx, dz = jnp.where(owner == 0, one, other), jnp.where(owner == 0, other, one)
            place[cell_number((x - dx) & (SIDE - 1), (z - dz) & (SIDE - 1), owner)] = done + u
        done += len(units)
    acc[...] = jnp.zeros_like(acc)
    copy.wait()

    for p in range(PANELS):
        for s in range(BANDS * SLOTS):
            source = (band - right_shifts[s // SLOTS]) & (BANDS - 1)
            panel = source * BLOCKS + ids[BANDS + s // SLOTS, GROUP * p + s % SLOTS]
            cell, j = panel // PANELS, panel % PANELS
            start = pl.multiple_of(place[cell] * UNIT + j * SLOTS * TILE, 16)
            product = jnp.dot(
                all_ref[pl.ds(start, SLOTS * TILE)], tiles_ref[p, s], preferred_element_type=jnp.float32
            )
            for k in range(SLOTS):
                block = ids[cell // GROUP, (cell % GROUP) * LANES + GROUP * j + k]
                acc[p, block] += product[k * TILE : (k + 1) * TILE]

    for p in range(PANELS):

        def add(r, total):
            value = acc[p, r]
            return total + jnp.sum((value * value).reshape(TILE // 8, 8, TILE), axis=0)

        total = lax.fori_loop(0, BLOCKS, add, jnp.zeros((8, TILE), jnp.float32), unroll=4)
        total = jnp.sum(total, axis=0, keepdims=True)
        for s, shift in enumerate(chunk_shifts):
            value = acc[p, kept_ref[p, 0, (band + shift) & (BANDS - 1)]]
            chunk_refs[s][p * TILE : (p + 1) * TILE] = value * value
            chunk_refs[s][PANELS * TILE + 4 * p : PANELS * TILE + 4 * p + 4] = jnp.broadcast_to(total, (4, TILE))


def finish_kernel(chunk_shifts, mask_ref, *refs):
    chunk_refs, out_ref = refs[:BANDS], refs[BANDS]
    band = lax.axis_index("layer")
    for p in range(PANELS):
        row = PANELS * TILE + 4 * p
        total = sum(ref[row : row + 1] for ref in chunk_refs)
        scale = (BANDS * BLOCKS * TILE) / total
        for s, shift in enumerate(chunk_shifts):
            source = (band - shift) & (BANDS - 1)
            keep = mask_ref[p, pl.ds(source, 1)].astype(jnp.float32).astype(jnp.bfloat16)
            value = (chunk_refs[s][p * TILE : (p + 1) * TILE] * scale).astype(jnp.bfloat16)
            out_ref[p, source, 0] = value * keep


def per_device(tile_values, band_rows, kept_rows, prune_mask):
    unit = jnp.concatenate([tile_values.reshape(BODY, TILE), id_rows(band_rows)], axis=0)
    rights = [lax.ppermute(unit, "layer", ring(s)) for s in (1, 3)]
    near, back, away = [along(unit, 0, shift) for shift in (2, 1, 3)]
    second = jnp.concatenate([back, away], axis=0)
    first, unit_again = pl.pallas_call(
        functools.partial(buffer_kernel, 2),
        out_shape=[jax.ShapeDtypeStruct((n * UNIT, TILE), jnp.bfloat16) for n in (2, 1)],
        in_specs=[VMEM] * 4,
        out_specs=[VMEM] * 2,
        compiler_params=LIMIT,
    )(unit, near, *rights)
    rights = [unit, *rights, lax.ppermute(unit_again, "layer", ring(2))]
    right_shifts = (0, 1, 3, 2)
    joined, tiles, right_ids = pl.pallas_call(
        functools.partial(join_kernel, 2),
        out_shape=[
            jax.ShapeDtypeStruct((SIDE * UNIT, TILE), jnp.bfloat16),
            jax.ShapeDtypeStruct((PANELS, BANDS * SLOTS, TILE, TILE), jnp.bfloat16),
            jax.ShapeDtypeStruct((BANDS, TILE), jnp.int32),
        ],
        in_specs=[VMEM] * (2 + BANDS),
        out_specs=[VMEM] * 3,
        compiler_params=LIMIT,
    )(first, second, *rights)
    up, down = along(first, 1, 1), along(first, 1, 3)
    up_b, down_b = along(second, 1, 1), along(second, 1, 3)
    fars = [along(up[:UNIT], 1, 1), along(down[UNIT:], 1, 3)]
    fars_b = [along(up_b[:UNIT], 1, 1), along(down_b[UNIT:], 1, 3)]
    one, two = (0, 2), (1, 3)
    parts = {
        "up": (up, [(a, 1) for a in one]),
        "down": (down, [(a, 3) for a in one]),
        "up_b": (up_b, [(a, 1) for a in two]),
        "down_b": (down_b, [(a, 3) for a in two]),
        "far_0": (fars[0], [(one[0], 2)]),
        "far_1": (fars[1], [(one[1], 2)]),
        "far_b0": (fars_b[0], [(two[0], 2)]),
        "far_b1": (fars_b[1], [(two[1], 2)]),
    }
    kept = [parts[name] for name in ("far_b0", "far_b1", "far_0", "far_1", "up_b", "down_b", "up", "down")]
    swapped = [parts[name] for name in ("up", "down", "up_b", "down_b", "far_b0", "far_b1", "far_0", "far_1")]
    line = [(first, [(a, 0) for a in one]), (second, [(a, 0) for a in two])]
    lefts = [one for one, _ in line + kept] + [swap(joined)] + [swap(part) for part, _ in swapped]
    origins = [[(a, b, False) for a, b in where] for _, where in line + kept]
    origins += [[(a, 0, True) for a in one + two]] + [[(a, b, True) for a, b in where] for _, where in swapped]
    counts = [len(where) for where in origins]
    units = sum(counts)
    chunk_shifts = (0, 1, 2, 3)
    chunks = pl.pallas_call(
        functools.partial(expand_kernel, origins, right_shifts, chunk_shifts),
        out_shape=[jax.ShapeDtypeStruct((CHUNK, TILE), jnp.float32)] * BANDS,
        in_specs=[SMEM] + [VMEM] * (len(lefts) + 2),
        out_specs=[VMEM] * BANDS,
        scratch_shapes=[
            pltpu.VMEM((units * UNIT, TILE), jnp.bfloat16),
            pltpu.VMEM((PANELS, BLOCKS, TILE, TILE), jnp.float32),
            pltpu.VMEM((2 * BANDS, TILE), jnp.int32),
            pltpu.SMEM((2 * BANDS, TILE), jnp.int32),
            pltpu.SMEM((units,), jnp.int32),
            pltpu.SemaphoreType.DMA,
        ],
        compiler_params=LIMIT,
        cost_estimate=pl.CostEstimate(flops=2**29, bytes_accessed=10 * 2**20, transcendentals=0),
    )(kept_rows, tiles, right_ids, *lefts)

    chunks = [chunks[0]] + [lax.ppermute(chunks[s], "layer", ring(chunk_shifts[s])) for s in (1, 2, 3)]
    return pl.pallas_call(
        functools.partial(finish_kernel, chunk_shifts),
        out_shape=jax.ShapeDtypeStruct((PANELS, BANDS, 1, TILE, TILE), jnp.bfloat16),
        in_specs=[VMEM] * (1 + BANDS),
        out_specs=VMEM,
        compiler_params=LIMIT,
    )(prune_mask, *chunks)


def solution(mesh):
    parts = Mesh(mesh.devices.reshape(SIDE, SIDE, 2, BANDS), CELL + ("layer",))
    return jax.shard_map(
        per_device,
        mesh=parts,
        in_specs=(
            P(CELL, "layer", None, None, None),
            P(CELL, "layer", None),
            P(CELL, "layer", None),
            P(CELL, None, None),
        ),
        out_specs=P(CELL, None, "layer", None, None),
        check_vma=False,
    )
```

```python
import functools

import jax
import jax.numpy as jnp
from jax import lax
from jax.experimental import pallas as pl
from jax.experimental.pallas import tpu as pltpu
from jax.sharding import Mesh, PartitionSpec as P

TILE = 128
SLOTS = 4
PANELS = 2
BANDS = 4
BLOCKS = 16
SIDE = 4
BODY = PANELS * SLOTS * TILE
UNIT = BODY + 16
CHUNK = PANELS * TILE + 8
GROUP = 8
LANES = TILE // GROUP
CELL = ("x", "z", "core")
VMEM = pl.BlockSpec(memory_space=pltpu.VMEM)
LIMIT = pltpu.CompilerParams(vmem_limit_bytes=40 * 1024 * 1024)


def ring(shift):
    return [(i, (i + shift) % SIDE) for i in range(SIDE)]


def cells(first, second):
    pairs = []
    for x in range(SIDE):
        for z in range(SIDE):
            for core, (dx, dz) in enumerate((first, second)):
                target = ((x + dx) % SIDE) * SIDE + (z + dz) % SIDE
                pairs.append(((x * SIDE + z) * 2 + core, target * 2 + core))
    return pairs


def along(value, axis, shift):
    steps = ((shift, 0), (0, shift))
    return lax.ppermute(value, CELL, cells(steps[axis], steps[1 - axis]))


def swap(value):
    return lax.ppermute(value, "core", [(0, 1), (1, 0)])


def cell_number(x, z, core):
    return (x * SIDE + z) * 2 + core


def id_rows(band_rows, kept_rows):
    cell = cell_number(*(lax.axis_index(name) for name in CELL))
    rows = jnp.concatenate([band_rows[:, 0], kept_rows[:, 0]], axis=1).reshape(1, LANES)
    row = lax.broadcasted_iota(jnp.int32, (16, TILE), 0)
    group = lax.broadcasted_iota(jnp.int32, (16, TILE), 1) // LANES
    here = ((row == cell // GROUP) & (group == cell % GROUP)) | ((row == GROUP) & (group == 0))
    return jnp.where(here, jnp.tile(rows, (1, GROUP)), 0).astype(jnp.bfloat16)


def buffer_kernel(count, *refs):
    unit_refs, (buffer_ref, again_ref) = refs[:count], refs[-2:]
    for u, ref in enumerate(unit_refs[1:] if count == 3 else unit_refs):
        buffer_ref[u * UNIT : (u + 1) * UNIT] = ref[...]
    again_ref[...] = unit_refs[0][...]


def join_kernel(count, *refs):
    line_refs, right_refs = refs[:count], refs[count : count + BANDS]
    line_ref, tiles_ref, ids_ref = refs[count + BANDS :]
    done = 0
    for ref in line_refs:
        line_ref[done : done + ref.shape[0]] = ref[...]
        done += ref.shape[0]
    for b, ref in enumerate(right_refs):
        ids_ref[b : b + 1] = ref[BODY:].astype(jnp.float32).astype(jnp.int32)[GROUP : GROUP + 1]
        for p in range(PANELS):
            tiles_ref[p, b * SLOTS : (b + 1) * SLOTS] = ref[p * SLOTS * TILE : (p + 1) * SLOTS * TILE].reshape(
                SLOTS, TILE, TILE
            )


def expand_kernel(origins, right_shifts, chunk_shifts, tiles_ref, right_ids_ref, *refs):
    left_refs, chunk_refs = refs[: len(origins)], refs[len(origins) : len(origins) + BANDS]
    all_ref, acc, table, ids, place, sem = refs[len(origins) + BANDS :]
    band, x, z, core = (lax.axis_index(name) for name in ("layer",) + CELL)

    sums, done = None, 0
    for ref, units in zip(left_refs, origins):
        for u in range(len(units)):
            block = ref[u * UNIT + BODY : (u + 1) * UNIT].astype(jnp.float32)
            sums = block if sums is None else sums + block
    table[: BANDS] = sums.astype(jnp.int32)[: BANDS]
    table[BANDS : 2 * BANDS] = right_ids_ref[...]
    copy = pltpu.make_async_copy(table, ids, sem)
    copy.start()
    for ref, units in zip(left_refs, origins):
        all_ref[done * UNIT : (done + len(units)) * UNIT] = ref[...]
        for u, (one, other, across) in enumerate(units):
            owner = 1 - core if across else core
            dx, dz = jnp.where(owner == 0, one, other), jnp.where(owner == 0, other, one)
            place[cell_number((x - dx) & (SIDE - 1), (z - dz) & (SIDE - 1), owner)] = done + u
        done += len(units)
    acc[...] = jnp.zeros_like(acc)
    copy.wait()

    for p in range(PANELS):
        for s in range(BANDS * SLOTS):
            source = (band - right_shifts[s // SLOTS]) & (BANDS - 1)
            panel = source * BLOCKS + ids[BANDS + s // SLOTS, GROUP * p + s % SLOTS]
            cell, j = panel // PANELS, panel % PANELS
            start = pl.multiple_of(place[cell] * UNIT + j * SLOTS * TILE, 16)
            product = jnp.dot(
                all_ref[pl.ds(start, SLOTS * TILE)], tiles_ref[p, s], preferred_element_type=jnp.float32
            )
            for k in range(SLOTS):
                block = ids[cell // GROUP, (cell % GROUP) * LANES + GROUP * j + k]
                acc[p, block] += product[k * TILE : (k + 1) * TILE]

    for p in range(PANELS):

        def add(r, total):
            value = acc[p, r]
            return total + jnp.sum((value * value).reshape(TILE // 8, 8, TILE), axis=0)

        total = lax.fori_loop(0, BLOCKS, add, jnp.zeros((8, TILE), jnp.float32), unroll=4)
        total = jnp.sum(total, axis=0, keepdims=True)
        for s, shift in enumerate(chunk_shifts):
            slot = (band + shift) & (BANDS - 1)
            value = acc[p, ids[BANDS, GROUP * p + SLOTS + slot]]
            chunk_refs[s][p * TILE : (p + 1) * TILE] = value * value
            chunk_refs[s][PANELS * TILE + 4 * p : PANELS * TILE + 4 * p + 4] = jnp.broadcast_to(total, (4, TILE))


def finish_kernel(chunk_shifts, mask_ref, *refs):
    chunk_refs, out_ref = refs[:BANDS], refs[BANDS]
    band = lax.axis_index("layer")
    for p in range(PANELS):
        row = PANELS * TILE + 4 * p
        total = sum(ref[row : row + 1] for ref in chunk_refs)
        scale = (BANDS * BLOCKS * TILE) / total
        for s, shift in enumerate(chunk_shifts):
            source = (band - shift) & (BANDS - 1)
            keep = mask_ref[p, pl.ds(source, 1)].astype(jnp.float32).astype(jnp.bfloat16)
            value = (chunk_refs[s][p * TILE : (p + 1) * TILE] * scale).astype(jnp.bfloat16)
            out_ref[p, source, 0] = value * keep


def per_device(tile_values, band_rows, kept_rows, prune_mask):
    unit = jnp.concatenate([tile_values.reshape(BODY, TILE), id_rows(band_rows, kept_rows)], axis=0)
    rights = [lax.ppermute(unit, "layer", ring(s)) for s in (1, 3)]
    near, back, away = [along(unit, 0, shift) for shift in (2, 1, 3)]
    second = jnp.concatenate([back, away], axis=0)
    first, unit_again = pl.pallas_call(
        functools.partial(buffer_kernel, 2),
        out_shape=[jax.ShapeDtypeStruct((n * UNIT, TILE), jnp.bfloat16) for n in (2, 1)],
        in_specs=[VMEM] * 4,
        out_specs=[VMEM] * 2,
        compiler_params=LIMIT,
    )(unit, near, *rights)
    rights = [unit, *rights, lax.ppermute(unit_again, "layer", ring(2))]
    right_shifts = (0, 1, 3, 2)
    joined, tiles, right_ids = pl.pallas_call(
        functools.partial(join_kernel, 2),
        out_shape=[
            jax.ShapeDtypeStruct((SIDE * UNIT, TILE), jnp.bfloat16),
            jax.ShapeDtypeStruct((PANELS, BANDS * SLOTS, TILE, TILE), jnp.bfloat16),
            jax.ShapeDtypeStruct((BANDS, TILE), jnp.int32),
        ],
        in_specs=[VMEM] * (2 + BANDS),
        out_specs=[VMEM] * 3,
        compiler_params=LIMIT,
    )(first, second, *rights)
    up, down = along(first, 1, 1), along(first, 1, 3)
    up_b, down_b = along(second, 1, 1), along(second, 1, 3)
    fars = [along(up[:UNIT], 1, 1), along(down[UNIT:], 1, 3)]
    fars_b = [along(up_b[:UNIT], 1, 1), along(down_b[UNIT:], 1, 3)]
    one, two = (0, 2), (1, 3)
    parts = {
        "up": (up, [(a, 1) for a in one]),
        "down": (down, [(a, 3) for a in one]),
        "up_b": (up_b, [(a, 1) for a in two]),
        "down_b": (down_b, [(a, 3) for a in two]),
        "far_0": (fars[0], [(one[0], 2)]),
        "far_1": (fars[1], [(one[1], 2)]),
        "far_b0": (fars_b[0], [(two[0], 2)]),
        "far_b1": (fars_b[1], [(two[1], 2)]),
    }
    kept = [parts[name] for name in ("far_b0", "far_b1", "far_0", "far_1", "up_b", "down_b", "up", "down")]
    swapped = [parts[name] for name in ("up", "down", "up_b", "down_b", "far_b0", "far_b1", "far_0", "far_1")]
    line = [(first, [(a, 0) for a in one]), (second, [(a, 0) for a in two])]
    lefts = [one for one, _ in line + kept] + [swap(joined)] + [swap(part) for part, _ in swapped]
    origins = [[(a, b, False) for a, b in where] for _, where in line + kept]
    origins += [[(a, 0, True) for a in one + two]] + [[(a, b, True) for a, b in where] for _, where in swapped]
    counts = [len(where) for where in origins]
    units = sum(counts)
    chunk_shifts = (0, 2, 1, 3)
    chunks = pl.pallas_call(
        functools.partial(expand_kernel, origins, right_shifts, chunk_shifts),
        out_shape=[jax.ShapeDtypeStruct((CHUNK, TILE), jnp.float32)] * BANDS,
        in_specs=[VMEM] * (len(lefts) + 2),
        out_specs=[VMEM] * BANDS,
        scratch_shapes=[
            pltpu.VMEM((units * UNIT, TILE), jnp.bfloat16),
            pltpu.VMEM((PANELS, BLOCKS, TILE, TILE), jnp.float32),
            pltpu.VMEM((2 * BANDS, TILE), jnp.int32),
            pltpu.SMEM((2 * BANDS, TILE), jnp.int32),
            pltpu.SMEM((units,), jnp.int32),
            pltpu.SemaphoreType.DMA,
        ],
        compiler_params=LIMIT,
        cost_estimate=pl.CostEstimate(flops=2**29, bytes_accessed=10 * 2**20, transcendentals=0),
    )(tiles, right_ids, *lefts)

    chunks = [chunks[0]] + [lax.ppermute(chunks[s], "layer", ring(chunk_shifts[s])) for s in (1, 2, 3)]
    return pl.pallas_call(
        functools.partial(finish_kernel, chunk_shifts),
        out_shape=jax.ShapeDtypeStruct((PANELS, BANDS, 1, TILE, TILE), jnp.bfloat16),
        in_specs=[VMEM] * (1 + BANDS),
        out_specs=VMEM,
        compiler_params=LIMIT,
    )(prune_mask, *chunks)


def solution(mesh):
    parts = Mesh(mesh.devices.reshape(SIDE, SIDE, 2, BANDS), CELL + ("layer",))
    return jax.shard_map(
        per_device,
        mesh=parts,
        in_specs=(
            P(CELL, "layer", None, None, None),
            P(CELL, "layer", None),
            P(CELL, "layer", None),
            P(CELL, None, None),
        ),
        out_specs=P(CELL, None, "layer", None, None),
        check_vma=False,
    )
```

```python
import functools

import jax
import jax.numpy as jnp
from jax import lax
from jax.experimental import pallas as pl
from jax.experimental.pallas import tpu as pltpu
from jax.sharding import Mesh, PartitionSpec as P

TILE = 128
SLOTS = 4
PANELS = 2
BANDS = 4
BLOCKS = 16
SIDE = 4
BODY = PANELS * SLOTS * TILE
UNIT = BODY + 16
CHUNK = PANELS * TILE + 8
GROUP = 8
LANES = TILE // GROUP
CELL = ("x", "z", "core")
VMEM = pl.BlockSpec(memory_space=pltpu.VMEM)
LIMIT = pltpu.CompilerParams(vmem_limit_bytes=40 * 1024 * 1024)


def ring(shift):
    return [(i, (i + shift) % SIDE) for i in range(SIDE)]


def cells(first, second):
    pairs = []
    for x in range(SIDE):
        for z in range(SIDE):
            for core, (dx, dz) in enumerate((first, second)):
                target = ((x + dx) % SIDE) * SIDE + (z + dz) % SIDE
                pairs.append(((x * SIDE + z) * 2 + core, target * 2 + core))
    return pairs


def along(value, axis, shift):
    steps = ((shift, 0), (0, shift))
    return lax.ppermute(value, CELL, cells(steps[axis], steps[1 - axis]))


def swap(value):
    return lax.ppermute(value, "core", [(0, 1), (1, 0)])


def cell_number(x, z, core):
    return (x * SIDE + z) * 2 + core


def id_rows(band_rows, kept_rows):
    cell = cell_number(*(lax.axis_index(name) for name in CELL))
    row = lax.broadcasted_iota(jnp.int32, (16, TILE), 0)
    lane = lax.broadcasted_iota(jnp.int32, (16, TILE), 1)
    group = lane // LANES
    here = ((row == cell // GROUP) & (group == cell % GROUP)) | ((row == GROUP) & (group == 0))
    shape = (16, TILE, PANELS, SLOTS)
    spot = lax.broadcasted_iota(jnp.int32, shape, 2) * GROUP + lax.broadcasted_iota(jnp.int32, shape, 3)
    place = (lane % LANES)[:, :, None, None]
    ids = jnp.where(place == spot, band_rows[:, 0], 0) + jnp.where(place == spot + SLOTS, kept_rows[:, 0], 0)
    return jnp.where(here, jnp.sum(ids, axis=(2, 3)), 0).astype(jnp.bfloat16)


def buffer_kernel(count, *refs):
    unit_refs, (buffer_ref, again_ref) = refs[:count], refs[-2:]
    for u, ref in enumerate(unit_refs[1:] if count == 3 else unit_refs):
        buffer_ref[u * UNIT : (u + 1) * UNIT] = ref[...]
    again_ref[...] = unit_refs[0][...]


def join_kernel(count, *refs):
    line_refs, right_refs = refs[:count], refs[count : count + BANDS]
    line_ref, tiles_ref, ids_ref = refs[count + BANDS :]
    done = 0
    for ref in line_refs:
        line_ref[done : done + ref.shape[0]] = ref[...]
        done += ref.shape[0]
    for b, ref in enumerate(right_refs):
        ids_ref[b : b + 1] = ref[BODY:].astype(jnp.float32).astype(jnp.int32)[GROUP : GROUP + 1]
        for p in range(PANELS):
            tiles_ref[p, b * SLOTS : (b + 1) * SLOTS] = ref[p * SLOTS * TILE : (p + 1) * SLOTS * TILE].reshape(
                SLOTS, TILE, TILE
            )


def expand_kernel(origins, right_shifts, chunk_shifts, tiles_ref, right_ids_ref, *refs):
    left_refs, chunk_refs = refs[: len(origins)], refs[len(origins) : len(origins) + BANDS]
    all_ref, acc, table, ids, place, sem = refs[len(origins) + BANDS :]
    band, x, z, core = (lax.axis_index(name) for name in ("layer",) + CELL)

    sums, done = None, 0
    for ref, units in zip(left_refs, origins):
        for u in range(len(units)):
            block = ref[u * UNIT + BODY : (u + 1) * UNIT].astype(jnp.float32)
            sums = block if sums is None else sums + block
    table[: BANDS] = sums.astype(jnp.int32)[: BANDS]
    table[BANDS : 2 * BANDS] = right_ids_ref[...]
    copy = pltpu.make_async_copy(table, ids, sem)
    copy.start()
    for ref, units in zip(left_refs, origins):
        all_ref[done * UNIT : (done + len(units)) * UNIT] = ref[...]
        for u, (one, other, across) in enumerate(units):
            owner = 1 - core if across else core
            dx, dz = jnp.where(owner == 0, one, other), jnp.where(owner == 0, other, one)
            place[cell_number((x - dx) & (SIDE - 1), (z - dz) & (SIDE - 1), owner)] = done + u
        done += len(units)
    acc[...] = jnp.zeros_like(acc)
    copy.wait()

    for p in range(PANELS):
        for s in range(BANDS * SLOTS):
            source = (band - right_shifts[s // SLOTS]) & (BANDS - 1)
            panel = source * BLOCKS + ids[BANDS + s // SLOTS, GROUP * p + s % SLOTS]
            cell, j = panel // PANELS, panel % PANELS
            start = pl.multiple_of(place[cell] * UNIT + j * SLOTS * TILE, 16)
            product = jnp.dot(
                all_ref[pl.ds(start, SLOTS * TILE)], tiles_ref[p, s], preferred_element_type=jnp.float32
            )
            for k in range(SLOTS):
                block = ids[cell // GROUP, (cell % GROUP) * LANES + GROUP * j + k]
                acc[p, block] += product[k * TILE : (k + 1) * TILE]

    for p in range(PANELS):

        def add(r, total):
            value = acc[p, r]
            return total + jnp.sum((value * value).reshape(TILE // 8, 8, TILE), axis=0)

        total = lax.fori_loop(0, BLOCKS, add, jnp.zeros((8, TILE), jnp.float32), unroll=4)
        total = jnp.sum(total, axis=0, keepdims=True)
        for s, shift in enumerate(chunk_shifts):
            slot = (band + shift) & (BANDS - 1)
            value = acc[p, ids[BANDS, GROUP * p + SLOTS + slot]]
            chunk_refs[s][p * TILE : (p + 1) * TILE] = value * value
            chunk_refs[s][PANELS * TILE + 4 * p : PANELS * TILE + 4 * p + 4] = jnp.broadcast_to(total, (4, TILE))


def finish_kernel(chunk_shifts, mask_ref, *refs):
    chunk_refs, out_ref = refs[:BANDS], refs[BANDS]
    band = lax.axis_index("layer")
    for p in range(PANELS):
        row = PANELS * TILE + 4 * p
        total = sum(ref[row : row + 1] for ref in chunk_refs)
        scale = (BANDS * BLOCKS * TILE) / total
        for s, shift in enumerate(chunk_shifts):
            source = (band - shift) & (BANDS - 1)
            keep = mask_ref[p, pl.ds(source, 1)].astype(jnp.float32).astype(jnp.bfloat16)
            value = (chunk_refs[s][p * TILE : (p + 1) * TILE] * scale).astype(jnp.bfloat16)
            out_ref[p, source, 0] = value * keep


def per_device(tile_values, band_rows, kept_rows, prune_mask):
    unit = jnp.concatenate([tile_values.reshape(BODY, TILE), id_rows(band_rows, kept_rows)], axis=0)
    rights = [lax.ppermute(unit, "layer", ring(s)) for s in (1, 3)]
    near, back, away = [along(unit, 0, shift) for shift in (2, 1, 3)]
    second = jnp.concatenate([back, away], axis=0)
    first, unit_again = pl.pallas_call(
        functools.partial(buffer_kernel, 2),
        out_shape=[jax.ShapeDtypeStruct((n * UNIT, TILE), jnp.bfloat16) for n in (2, 1)],
        in_specs=[VMEM] * 4,
        out_specs=[VMEM] * 2,
        compiler_params=LIMIT,
    )(unit, near, *rights)
    rights = [unit, *rights, lax.ppermute(unit_again, "layer", ring(2))]
    right_shifts = (0, 1, 3, 2)
    joined, tiles, right_ids = pl.pallas_call(
        functools.partial(join_kernel, 2),
        out_shape=[
            jax.ShapeDtypeStruct((SIDE * UNIT, TILE), jnp.bfloat16),
            jax.ShapeDtypeStruct((PANELS, BANDS * SLOTS, TILE, TILE), jnp.bfloat16),
            jax.ShapeDtypeStruct((BANDS, TILE), jnp.int32),
        ],
        in_specs=[VMEM] * (2 + BANDS),
        out_specs=[VMEM] * 3,
        compiler_params=LIMIT,
    )(first, second, *rights)
    up, down = along(first, 1, 1), along(first, 1, 3)
    up_b, down_b = along(second, 1, 1), along(second, 1, 3)
    fars = [along(up[:UNIT], 1, 1), along(down[UNIT:], 1, 3)]
    fars_b = [along(up_b[:UNIT], 1, 1), along(down_b[UNIT:], 1, 3)]
    one, two = (0, 2), (1, 3)
    parts = {
        "up": (up, [(a, 1) for a in one]),
        "down": (down, [(a, 3) for a in one]),
        "up_b": (up_b, [(a, 1) for a in two]),
        "down_b": (down_b, [(a, 3) for a in two]),
        "far_0": (fars[0], [(one[0], 2)]),
        "far_1": (fars[1], [(one[1], 2)]),
        "far_b0": (fars_b[0], [(two[0], 2)]),
        "far_b1": (fars_b[1], [(two[1], 2)]),
    }
    kept = [parts[name] for name in ("far_b0", "far_b1", "far_0", "far_1", "up_b", "down_b", "up", "down")]
    swapped = [parts[name] for name in ("up", "down", "up_b", "down_b", "far_b0", "far_b1", "far_0", "far_1")]
    line = [(first, [(a, 0) for a in one]), (second, [(a, 0) for a in two])]
    lefts = [one for one, _ in line + kept] + [swap(joined)] + [swap(part) for part, _ in swapped]
    origins = [[(a, b, False) for a, b in where] for _, where in line + kept]
    origins += [[(a, 0, True) for a in one + two]] + [[(a, b, True) for a, b in where] for _, where in swapped]
    counts = [len(where) for where in origins]
    units = sum(counts)
    chunk_shifts = (0, 2, 1, 3)
    chunks = pl.pallas_call(
        functools.partial(expand_kernel, origins, right_shifts, chunk_shifts),
        out_shape=[jax.ShapeDtypeStruct((CHUNK, TILE), jnp.float32)] * BANDS,
        in_specs=[VMEM] * (len(lefts) + 2),
        out_specs=[VMEM] * BANDS,
        scratch_shapes=[
            pltpu.VMEM((units * UNIT, TILE), jnp.bfloat16),
            pltpu.VMEM((PANELS, BLOCKS, TILE, TILE), jnp.float32),
            pltpu.VMEM((2 * BANDS, TILE), jnp.int32),
            pltpu.SMEM((2 * BANDS, TILE), jnp.int32),
            pltpu.SMEM((units,), jnp.int32),
            pltpu.SemaphoreType.DMA,
        ],
        compiler_params=LIMIT,
        cost_estimate=pl.CostEstimate(flops=2**29, bytes_accessed=10 * 2**20, transcendentals=0),
    )(tiles, right_ids, *lefts)

    chunks = [chunks[0]] + [lax.ppermute(chunks[s], "layer", ring(chunk_shifts[s])) for s in (1, 2, 3)]
    return pl.pallas_call(
        functools.partial(finish_kernel, chunk_shifts),
        out_shape=jax.ShapeDtypeStruct((PANELS, BANDS, 1, TILE, TILE), jnp.bfloat16),
        in_specs=[VMEM] * (1 + BANDS),
        out_specs=VMEM,
        compiler_params=LIMIT,
    )(prune_mask, *chunks)


def solution(mesh):
    parts = Mesh(mesh.devices.reshape(SIDE, SIDE, 2, BANDS), CELL + ("layer",))
    return jax.shard_map(
        per_device,
        mesh=parts,
        in_specs=(
            P(CELL, "layer", None, None, None),
            P(CELL, "layer", None),
            P(CELL, "layer", None),
            P(CELL, None, None),
        ),
        out_specs=P(CELL, None, "layer", None, None),
        check_vma=False,
    )
```

```python
import functools

import jax
import jax.numpy as jnp
from jax import lax
from jax.experimental import pallas as pl
from jax.experimental.pallas import tpu as pltpu
from jax.sharding import Mesh, PartitionSpec as P

TILE = 128
SLOTS = 4
PANELS = 2
BANDS = 4
BLOCKS = 16
SIDE = 4
BODY = PANELS * SLOTS * TILE
UNIT = BODY + 16
CHUNK = PANELS * TILE + 8
GROUP = 8
LANES = TILE // GROUP
CELL = ("x", "z", "core")
VMEM = pl.BlockSpec(memory_space=pltpu.VMEM)
LIMIT = pltpu.CompilerParams(vmem_limit_bytes=40 * 1024 * 1024)


def ring(shift):
    return [(i, (i + shift) % SIDE) for i in range(SIDE)]


def cells(first, second):
    pairs = []
    for x in range(SIDE):
        for z in range(SIDE):
            for core, (dx, dz) in enumerate((first, second)):
                target = ((x + dx) % SIDE) * SIDE + (z + dz) % SIDE
                pairs.append(((x * SIDE + z) * 2 + core, target * 2 + core))
    return pairs


def along(value, axis, shift):
    steps = ((shift, 0), (0, shift))
    return lax.ppermute(value, CELL, cells(steps[axis], steps[1 - axis]))


def swap(value):
    return lax.ppermute(value, "core", [(0, 1), (1, 0)])


def cell_number(x, z, core):
    return (x * SIDE + z) * 2 + core


def id_rows(band_rows, kept_rows):
    cell = cell_number(*(lax.axis_index(name) for name in CELL))
    row = lax.broadcasted_iota(jnp.int32, (16, TILE), 0)
    lane = lax.broadcasted_iota(jnp.int32, (16, TILE), 1)
    group = lane // LANES
    here = ((row == cell // GROUP) & (group == cell % GROUP)) | ((row == GROUP) & (group == 0))
    shape = (16, TILE, PANELS, SLOTS)
    spot = lax.broadcasted_iota(jnp.int32, shape, 2) * GROUP + lax.broadcasted_iota(jnp.int32, shape, 3)
    place = (lane % LANES)[:, :, None, None]
    ids = jnp.where(place == spot, band_rows[:, 0], 0) + jnp.where(place == spot + SLOTS, kept_rows[:, 0], 0)
    return jnp.where(here, jnp.sum(ids, axis=(2, 3)), 0).astype(jnp.bfloat16)


def buffer_kernel(count, *refs):
    unit_refs, (buffer_ref, again_ref) = refs[:count], refs[-2:]
    for u, ref in enumerate(unit_refs[1:] if count == 3 else unit_refs):
        buffer_ref[u * UNIT : (u + 1) * UNIT] = ref[...]
    again_ref[...] = unit_refs[0][...]


def join_kernel(count, *refs):
    line_refs, right_refs = refs[:count], refs[count : count + BANDS]
    line_ref, tiles_ref, ids_ref = refs[count + BANDS :]
    done = 0
    for ref in line_refs:
        line_ref[done : done + ref.shape[0]] = ref[...]
        done += ref.shape[0]
    for b, ref in enumerate(right_refs):
        ids_ref[b : b + 1] = ref[BODY:].astype(jnp.float32).astype(jnp.int32)[GROUP : GROUP + 1]
        for p in range(PANELS):
            tiles_ref[p, b * SLOTS : (b + 1) * SLOTS] = ref[p * SLOTS * TILE : (p + 1) * SLOTS * TILE].reshape(
                SLOTS, TILE, TILE
            )


def expand_kernel(origins, right_shifts, chunk_shifts, tiles_ref, right_ids_ref, *refs):
    left_refs, chunk_refs = refs[: len(origins)], refs[len(origins) : len(origins) + BANDS]
    all_ref, acc, table, ids, place, sem = refs[len(origins) + BANDS :]
    band, x, z, core = (lax.axis_index(name) for name in ("layer",) + CELL)

    sums, done = None, 0
    for ref, units in zip(left_refs, origins):
        for u in range(len(units)):
            block = ref[u * UNIT + BODY : (u + 1) * UNIT].astype(jnp.float32)
            sums = block if sums is None else sums + block
    table[: BANDS] = sums.astype(jnp.int32)[: BANDS]
    table[BANDS : 2 * BANDS] = right_ids_ref[...]
    copy = pltpu.make_async_copy(table, ids, sem)
    copy.start()
    for ref, units in zip(left_refs, origins):
        all_ref[done * UNIT : (done + len(units)) * UNIT] = ref[...]
        for u, (one, other, across) in enumerate(units):
            owner = 1 - core if across else core
            dx, dz = jnp.where(owner == 0, one, other), jnp.where(owner == 0, other, one)
            place[cell_number((x - dx) & (SIDE - 1), (z - dz) & (SIDE - 1), owner)] = done + u
        done += len(units)
    acc[...] = jnp.zeros_like(acc)
    copy.wait()

    for p in range(PANELS):
        for s in range(BANDS * SLOTS):
            source = (band - right_shifts[s // SLOTS]) & (BANDS - 1)
            panel = source * BLOCKS + ids[BANDS + s // SLOTS, GROUP * p + s % SLOTS]
            cell, j = panel // PANELS, panel % PANELS
            start = pl.multiple_of(place[cell] * UNIT + j * SLOTS * TILE, 16)
            product = jnp.dot(
                all_ref[pl.ds(start, SLOTS * TILE)], tiles_ref[p, s], preferred_element_type=jnp.float32
            )
            for k in range(SLOTS):
                block = ids[cell // GROUP, (cell % GROUP) * LANES + GROUP * j + k]
                acc[p, block] += product[k * TILE : (k + 1) * TILE]

    for p in range(PANELS):

        def add(r, total):
            value = acc[p, r]
            return total + jnp.sum((value * value).reshape(TILE // 8, 8, TILE), axis=0)

        total = lax.fori_loop(0, BLOCKS, add, jnp.zeros((8, TILE), jnp.float32), unroll=BLOCKS)
        total = jnp.sum(total, axis=0, keepdims=True)
        for s, shift in enumerate(chunk_shifts):
            slot = (band + shift) & (BANDS - 1)
            value = acc[p, ids[BANDS, GROUP * p + SLOTS + slot]]
            chunk_refs[s][p * TILE : (p + 1) * TILE] = value * value
            chunk_refs[s][PANELS * TILE + 4 * p : PANELS * TILE + 4 * p + 4] = jnp.broadcast_to(total, (4, TILE))


def finish_kernel(chunk_shifts, mask_ref, *refs):
    chunk_refs, out_ref = refs[:BANDS], refs[BANDS]
    band = lax.axis_index("layer")
    for p in range(PANELS):
        row = PANELS * TILE + 4 * p
        total = sum(ref[row : row + 1] for ref in chunk_refs)
        scale = (BANDS * BLOCKS * TILE) / total
        for s, shift in enumerate(chunk_shifts):
            source = (band - shift) & (BANDS - 1)
            keep = mask_ref[p, pl.ds(source, 1)].astype(jnp.float32).astype(jnp.bfloat16)
            value = (chunk_refs[s][p * TILE : (p + 1) * TILE] * scale).astype(jnp.bfloat16)
            out_ref[p, source, 0] = value * keep


def per_device(tile_values, band_rows, kept_rows, prune_mask):
    unit = jnp.concatenate([tile_values.reshape(BODY, TILE), id_rows(band_rows, kept_rows)], axis=0)
    rights = [lax.ppermute(unit, "layer", ring(s)) for s in (1, 3)]
    near, back, away = [along(unit, 0, shift) for shift in (2, 1, 3)]
    second = jnp.concatenate([back, away], axis=0)
    first, unit_again = pl.pallas_call(
        functools.partial(buffer_kernel, 2),
        out_shape=[jax.ShapeDtypeStruct((n * UNIT, TILE), jnp.bfloat16) for n in (2, 1)],
        in_specs=[VMEM] * 4,
        out_specs=[VMEM] * 2,
        compiler_params=LIMIT,
    )(unit, near, *rights)
    rights = [unit, *rights, lax.ppermute(unit_again, "layer", ring(2))]
    right_shifts = (0, 1, 3, 2)
    joined, tiles, right_ids = pl.pallas_call(
        functools.partial(join_kernel, 2),
        out_shape=[
            jax.ShapeDtypeStruct((SIDE * UNIT, TILE), jnp.bfloat16),
            jax.ShapeDtypeStruct((PANELS, BANDS * SLOTS, TILE, TILE), jnp.bfloat16),
            jax.ShapeDtypeStruct((BANDS, TILE), jnp.int32),
        ],
        in_specs=[VMEM] * (2 + BANDS),
        out_specs=[VMEM] * 3,
        compiler_params=LIMIT,
    )(first, second, *rights)
    up, down = along(first, 1, 1), along(first, 1, 3)
    up_b, down_b = along(second, 1, 1), along(second, 1, 3)
    fars = [along(up[:UNIT], 1, 1), along(down[UNIT:], 1, 3)]
    fars_b = [along(up_b[:UNIT], 1, 1), along(down_b[UNIT:], 1, 3)]
    one, two = (0, 2), (1, 3)
    parts = {
        "up": (up, [(a, 1) for a in one]),
        "down": (down, [(a, 3) for a in one]),
        "up_b": (up_b, [(a, 1) for a in two]),
        "down_b": (down_b, [(a, 3) for a in two]),
        "far_0": (fars[0], [(one[0], 2)]),
        "far_1": (fars[1], [(one[1], 2)]),
        "far_b0": (fars_b[0], [(two[0], 2)]),
        "far_b1": (fars_b[1], [(two[1], 2)]),
    }
    kept = [parts[name] for name in ("far_b0", "far_b1", "far_0", "far_1", "up_b", "down_b", "up", "down")]
    swapped = [parts[name] for name in ("up", "down", "up_b", "down_b", "far_b0", "far_b1", "far_0", "far_1")]
    line = [(first, [(a, 0) for a in one]), (second, [(a, 0) for a in two])]
    lefts = [one for one, _ in line + kept] + [swap(joined)] + [swap(part) for part, _ in swapped]
    origins = [[(a, b, False) for a, b in where] for _, where in line + kept]
    origins += [[(a, 0, True) for a in one + two]] + [[(a, b, True) for a, b in where] for _, where in swapped]
    counts = [len(where) for where in origins]
    units = sum(counts)
    chunk_shifts = (0, 2, 1, 3)
    chunks = pl.pallas_call(
        functools.partial(expand_kernel, origins, right_shifts, chunk_shifts),
        out_shape=[jax.ShapeDtypeStruct((CHUNK, TILE), jnp.float32)] * BANDS,
        in_specs=[VMEM] * (len(lefts) + 2),
        out_specs=[VMEM] * BANDS,
        scratch_shapes=[
            pltpu.VMEM((units * UNIT, TILE), jnp.bfloat16),
            pltpu.VMEM((PANELS, BLOCKS, TILE, TILE), jnp.float32),
            pltpu.VMEM((2 * BANDS, TILE), jnp.int32),
            pltpu.SMEM((2 * BANDS, TILE), jnp.int32),
            pltpu.SMEM((units,), jnp.int32),
            pltpu.SemaphoreType.DMA,
        ],
        compiler_params=LIMIT,
        cost_estimate=pl.CostEstimate(flops=2**29, bytes_accessed=10 * 2**20, transcendentals=0),
    )(tiles, right_ids, *lefts)

    chunks = [chunks[0]] + [lax.ppermute(chunks[s], "layer", ring(chunk_shifts[s])) for s in (1, 2, 3)]
    return pl.pallas_call(
        functools.partial(finish_kernel, chunk_shifts),
        out_shape=jax.ShapeDtypeStruct((PANELS, BANDS, 1, TILE, TILE), jnp.bfloat16),
        in_specs=[VMEM] * (1 + BANDS),
        out_specs=VMEM,
        compiler_params=LIMIT,
    )(prune_mask, *chunks)


def solution(mesh):
    parts = Mesh(mesh.devices.reshape(SIDE, SIDE, 2, BANDS), CELL + ("layer",))
    return jax.shard_map(
        per_device,
        mesh=parts,
        in_specs=(
            P(CELL, "layer", None, None, None),
            P(CELL, "layer", None),
            P(CELL, "layer", None),
            P(CELL, None, None),
        ),
        out_specs=P(CELL, None, "layer", None, None),
        check_vma=False,
    )
```
